256 devices in a mesh: row: 8 (over z_lo, x), col: 32 (over z_hi, y, core).
Axes of the slice: x: 4, y: 4, z: 8 (z_hi: 4, z_lo: 2; z = z_hi * 2 + z_lo), core: 2. Of those that a mesh axis runs over, the one named last changes fastest.
Arguments:
- obj_start: float32 [2, 2048, 8192], P(None, 'row', 'col'), may hold values from -4 to 4
- probe_start: float32 [2, 128, 128], replicated, may hold values from -4 to 4
- amplitudes: bfloat16 [8, 32, 32, 128, 128], P('row', 'col'), may hold values from 0 to 2
- centres: int32 [2, 8, 32, 32], P(None, 'row', 'col'), may hold values from 0 to 255
- members: int32 [2, 8, 32, 32], P(None, 'row', 'col'), may hold values from 0 to 1, as said below
Outputs:
- obj_out: float32 [2, 2048, 8192], P(None, 'row', 'col')
- probe_out: float32 [2, 128, 128], replicated
The draws below stay inside these ranges and needn't reach their ends.
Inputs may be any that keep to these rules, and one draw needn't show every extreme that they name: A slot belongs to at most one iteration's minibatch. In each iteration a device has at most 16 members, and some device has exactly 16 in every iteration.
All inputs are finite; a program needn't handle non-finite values.
Results may differ from the reference program's by a relative error of at most 0.0003.
Values sent between devices are 32-bit elements; how exact they have to be, the bound alone decides.
No kernel may reach another device: no remote copies, remote signals or barrier semaphores. Data moves between devices by JAX's collectives and lax.ppermute only.
A program may use at most 128 MiB of HBM per device.

```python
import jax
import jax.numpy as jnp
from jax import lax

WIN = 128
TILE = 256
CAP = 32
ITERS = 2
GRID_R = 8
GRID_C = 32
NY = 2048
NX = 8192


def draw_members(key, part):
    key = jax.random.fold_in(key, 7)
    key_live, key_perm, key_full = jax.random.split(key, 3)
    count = GRID_R * GRID_C
    live = jax.random.randint(key_live, (count,), CAP // 4, CAP + 1)
    full = jax.random.randint(key_full, (), 0, count)
    live = jnp.where(jnp.arange(count) == full, CAP, live)
    keys = jax.random.split(key_perm, count)
    ranks = jax.vmap(lambda k: jax.random.permutation(k, CAP))(keys)
    which = ranks * ITERS // jnp.maximum(live, 1)[:, None]
    alive = ranks < live[:, None]
    layers = [(alive & (which == t)).astype(jnp.int32) for t in range(ITERS)]
    return jnp.stack(layers).reshape(ITERS, GRID_R, GRID_C, CAP)


def touch_ends(result, key, smallest, high):
    longest = result.shape.index(max(result.shape))
    spots = []
    for shift in (0, 1):
        where = [jax.random.randint(jax.random.fold_in(key, axis), (), 0, length) for axis, length in enumerate(result.shape)]
        where[longest] = (where[longest] + shift) % result.shape[longest]
        spots.append(tuple(where))
    return result.at[spots[0]].set(smallest).at[spots[1]].set(high)


def levels(key, shape, cuts, low, top_value):
    def one(axis_at, parts):
        heights = jax.random.uniform(jax.random.fold_in(jax.random.fold_in(key, 6), axis_at), (parts,), jnp.float32, low / len(cuts), top_value / len(cuts))
        return jnp.repeat(jnp.exp(heights), shape[axis_at] // parts).reshape((-1,) + (1,) * (len(shape) - axis_at - 1))

    gain = one(*cuts[0])
    for cut in cuts[1:]:
        gain = gain * one(*cut)
    return gain


def bell_draw(own_key, dims, scale, limit, shards=(), held_as=jnp.bfloat16):
    array = jax.random.normal(own_key, dims, jnp.float32) * scale
    if len(shards) > 0:
        array = levels(own_key, dims, shards, -0.22, 0.18) * array
    return jnp.clip(array, min=-limit, max=limit).astype(held_as)


def setup_inputs(seed: int = 0) -> dict:
    key_list = jax.random.split(jax.random.key(seed), 6)
    return {
        "obj_start": bell_draw(key_list[0], (2, NY, NX), 0.7, 4.0, ((1, 8), (2, 32)), jnp.float32),
        "probe_start": bell_draw(key_list[1], (2, WIN, WIN), 0.7, 4.0, (), jnp.float32),
        "amplitudes": jnp.clip(2.0 * jax.random.uniform(key_list[2], (GRID_R, GRID_C, CAP, WIN, WIN), jnp.float32) ** levels(key_list[2], (GRID_R, GRID_C, CAP, WIN, WIN), ((0, 8), (1, 32)), -0.2, 0.2), 0.0, 2.0).astype(jnp.bfloat16),
        "centres": touch_ends(jax.random.randint(key_list[3], (2, GRID_R, GRID_C, CAP), 0, TILE), jax.random.fold_in(key_list[3], 1), 0, TILE - 1).astype(jnp.int32),
        "members": draw_members(jax.random.fold_in(key_list[5], 71), 0),
    }


def reference(obj_start, probe_start, amplitudes, centres, members):
    rim = WIN // 2
    tops = (centres[0] + (jnp.arange(GRID_R, dtype=jnp.int32) * TILE)[:, None, None]).reshape(-1).astype(jnp.int32)
    lefts = (centres[1] + (jnp.arange(GRID_C, dtype=jnp.int32) * TILE)[None, :, None]).reshape(-1).astype(jnp.int32)
    amp_all = amplitudes.reshape(-1, WIN, WIN)
    obj = obj_start
    probe = probe_start
    for step in range(ITERS):
        weights = members[step].reshape(-1).astype(jnp.float32)
        padded = jnp.pad(obj, ((0, 0), (rim, rim), (rim, rim)))
        probe_c = probe[0] + 1j * probe[1]

        def visit(carry, item):
            acc, grad_p, weight_p = carry
            top, left, amp_one, wt = item
            start = (jnp.int32(0), top, left)
            patch = lax.dynamic_slice(padded, start, (2, WIN, WIN))
            obj_c = patch[0] + 1j * patch[1]
            big = jnp.fft.fft2(probe_c * obj_c, norm="ortho")
            mag = jnp.maximum(jnp.abs(big), 0.5)
            chi = big * ((1.0 - amp_one.astype(jnp.float32) / mag) * wt)
            back = jnp.fft.ifft2(chi, norm="ortho")
            grad_o = jnp.conj(probe_c) * back
            current = lax.dynamic_slice(acc, start, (2, WIN, WIN))
            acc = lax.dynamic_update_slice(acc, current + jnp.stack([grad_o.real, grad_o.imag]), start)
            term = jnp.conj(obj_c) * back
            grad_p = grad_p + jnp.stack([term.real, term.imag])
            weight_p = weight_p + wt * (patch[0] * patch[0] + patch[1] * patch[1])
            return (acc, grad_p, weight_p), None

        init = (jnp.zeros_like(padded), jnp.zeros_like(probe), jnp.zeros_like(probe[0]))
        (acc, grad_p, weight_p), unused = lax.scan(visit, init, (tops, lefts, amp_all, weights))
        grad_obj = acc[:, rim:rim + NY, rim:rim + NX]
        peak = jnp.max(probe[0] * probe[0] + probe[1] * probe[1])
        obj = obj - grad_obj / (peak + 1e-6)
        probe = probe - grad_p / (weight_p + 1e-6)
    return obj, probe
```

```python
import functools
import math

import jax
import jax.numpy as jnp
import numpy as np
from jax import lax
from jax.experimental import pallas as pl
from jax.experimental.pallas import tpu as pltpu
from jax.sharding import PartitionSpec as P

WIDTH = 128
RIM = WIDTH // 2
TILE = 256
EXT = TILE + WIDTH
BLOCKS = EXT // WIDTH
VMEM_LIMIT = 56 * 1024 * 1024


def dft_tables():
    index = np.arange(WIDTH)
    angle = (np.outer(index, index) % WIDTH) * (2.0 * math.pi / WIDTH)
    cos_t = np.cos(angle) / math.sqrt(WIDTH)
    sin_t = np.sin(angle) / math.sqrt(WIDTH)
    ahead = np.block([[cos_t, -sin_t], [sin_t, cos_t]])
    back = np.block([[cos_t, sin_t], [-sin_t, cos_t]])
    out = []
    for table in (ahead, back):
        high = table.astype(jnp.bfloat16)
        low = (table - high.astype(np.float64)).astype(jnp.bfloat16)
        out.append((high, low))
    (ah, al), (bh, bl) = out
    right_a = np.concatenate([ah, ah, al], 0)
    right_b = np.concatenate([bh, bh, bl], 0)
    left_a = np.concatenate([ah, ah, al], 1)
    left_b = np.concatenate([bh, bh, bl], 1)
    return right_a, left_b, left_a, right_b


def split(value):
    high = value.astype(jnp.bfloat16)
    low = (value - high.astype(jnp.float32)).astype(jnp.bfloat16)
    return high, low


def times_right(value, table):
    high, low = split(value)
    return jnp.dot(
        jnp.concatenate([high, low, high], 1), table, preferred_element_type=jnp.float32
    )


def times_left(table, value):
    high, low = split(value)
    return jnp.dot(
        table, jnp.concatenate([high, low, high], 0), preferred_element_type=jnp.float32
    )


def swap_halves(value):
    top, bottom = value[:WIDTH], value[WIDTH:]
    return jnp.concatenate(
        [
            jnp.concatenate([top[:, :WIDTH], bottom[:, :WIDTH]], 1),
            jnp.concatenate([top[:, WIDTH:], bottom[:, WIDTH:]], 1),
        ],
        0,
    )


def patterns_kernel(
    flags_ref, rows_ref, cols_ref, ext_ref, probe_ref, amp_ref,
    ra_ref, lb_ref, la_ref, rb_ref,
    acc_ref, sums_ref, slots_ref,
):
    cap = flags_ref.shape[0]
    slots_ref[0] = 0

    def note(slot, count):
        @pl.when(flags_ref[slot] != 0)
        def _():
            slots_ref[count] = slot

        return count + (flags_ref[slot] != 0).astype(jnp.int32)

    count = lax.fori_loop(0, cap, note, jnp.int32(0))
    acc_ref[...] = jnp.zeros_like(acc_ref)
    sums_ref[...] = jnp.zeros_like(sums_ref)
    lane = lax.broadcasted_iota(jnp.int32, (WIDTH, WIDTH), 1)

    def where_is(slot):
        left = cols_ref[slot]
        block = left // WIDTH
        return rows_ref[slot], block, left - block * WIDTH

    def patch(slot):
        top, block, shift = where_is(slot)
        parts = []
        for part in range(2):
            near = ext_ref[part, block, pl.ds(top, WIDTH), :]
            far = ext_ref[part, block + 1, pl.ds(top, WIDTH), :]
            merged = jnp.where(lane >= shift, near, far)
            parts.append(pltpu.roll(merged, (WIDTH - shift) % WIDTH, 1))
        return parts

    def place(slot, update):
        top, block, shift = where_is(slot)
        for part in range(2):
            rolled = pltpu.roll(update[part], shift, 1)
            acc_ref[part, block, pl.ds(top, WIDTH), :] += jnp.where(lane >= shift, rolled, 0.0)
            acc_ref[part, block + 1, pl.ds(top, WIDTH), :] += jnp.where(lane < shift, rolled, 0.0)

    def pair(index, carry):
        first = slots_ref[2 * index]
        real = 2 * index + 1 < count
        second = jnp.where(real, slots_ref[jnp.minimum(2 * index + 1, count - 1)], first)
        keep = real.astype(jnp.float32)
        pr, pi = probe_ref[0], probe_ref[1]
        waves = []
        objs = []
        for slot in (first, second):
            obj_re, obj_im = patch(slot)
            objs.append((obj_re, obj_im))
            waves.append(
                jnp.concatenate([pr * obj_re - pi * obj_im, pr * obj_im + pi * obj_re], 1)
            )
        field = times_right(jnp.concatenate(waves, 0), ra_ref[...])
        field = times_left(lb_ref[...], swap_halves(field))
        big_re, big_im = field[:WIDTH], field[WIDTH:]
        amp = jnp.concatenate(
            [amp_ref[first].astype(jnp.float32), amp_ref[second].astype(jnp.float32)], 1
        )
        inverse = jnp.minimum(lax.rsqrt(big_re * big_re + big_im * big_im), 2.0)
        factor = 1.0 - amp * inverse
        factor = jnp.concatenate([factor[:, :WIDTH], factor[:, WIDTH:] * keep], 1)
        chi = jnp.concatenate([big_re * factor, big_im * factor], 0)
        field = times_left(la_ref[...], chi)
        field = times_right(swap_halves(field), rb_ref[...])
        grads = [jnp.zeros((WIDTH, WIDTH), jnp.float32)] * 2
        weight = None
        for which, slot in enumerate((first, second)):
            part = field[which * WIDTH : (which + 1) * WIDTH]
            back_re, back_im = part[:, :WIDTH], part[:, WIDTH:]
            obj_re, obj_im = objs[which]
            place(slot, (pr * back_re + pi * back_im, pr * back_im - pi * back_re))
            grads[0] = grads[0] + (obj_re * back_re + obj_im * back_im)
            grads[1] = grads[1] + (obj_re * back_im - obj_im * back_re)
            power = obj_re * obj_re + obj_im * obj_im
            weight = power if weight is None else weight + keep * power
        sums_ref[0] += grads[0]
        sums_ref[1] += grads[1]
        sums_ref[2] += weight
        return carry

    lax.fori_loop(0, (count + 1) // 2, pair, jnp.int32(0))


def patterns(flags, rows, cols, ext, probe, amp, tables):
    smem = pl.BlockSpec(memory_space=pltpu.SMEM)
    vmem = pl.BlockSpec(memory_space=pltpu.VMEM)
    return pl.pallas_call(
        patterns_kernel,
        out_shape=(
            jax.ShapeDtypeStruct(ext.shape, jnp.float32),
            jax.ShapeDtypeStruct((3, WIDTH, WIDTH), jnp.float32),
        ),
        in_specs=[smem] * 3 + [vmem] * 7,
        out_specs=(vmem, vmem),
        scratch_shapes=[pltpu.SMEM((flags.shape[0],), jnp.int32)],
        compiler_params=pltpu.CompilerParams(vmem_limit_bytes=VMEM_LIMIT),
        name="patterns",
    )(flags, rows, cols, ext, probe, amp, *tables)


def edges(rows, cols):
    row = lax.axis_index("row")
    col = lax.axis_index("col")
    return jnp.stack([row > 0, row < rows - 1, col > 0, col < cols - 1]).astype(jnp.int32)


def assemble_kernel(edge_ref, obj_ref, up, down, left, right, ul, ur, dl, dr, ext_ref):
    lane = lax.broadcasted_iota(jnp.int32, (RIM, WIDTH), 1)
    low = lane < RIM
    has_up, has_down = edge_ref[0] != 0, edge_ref[1] != 0
    has_left, has_right = edge_ref[2] != 0, edge_ref[3] != 0

    def half(value):
        return pltpu.roll(value, RIM, 1)

    def gate(value, *conditions):
        for condition in conditions:
            value = jnp.where(condition, value, 0.0)
        return value

    def store(part, rows, mid, west, east):
        a, b = mid[:, :WIDTH], mid[:, WIDTH:]
        ra, rb = half(a), half(b)
        ext_ref[part, 0, rows, :] = jnp.where(low, west, ra)
        ext_ref[part, 1, rows, :] = jnp.where(low, ra, rb)
        ext_ref[part, 2, rows, :] = jnp.where(low, rb, half(east))

    for part in range(2):
        store(
            part, pl.ds(0, RIM), gate(up[part], has_up),
            gate(ul[part], has_up, has_left), gate(ur[part], has_up, has_right),
        )
        store(
            part, pl.ds(RIM + TILE, RIM), gate(down[part], has_down),
            gate(dl[part], has_down, has_left), gate(dr[part], has_down, has_right),
        )
        for step in range(TILE // RIM):
            rows = pl.ds((step % 2) * RIM, RIM)
            west = left[part, rows, :]
            east = right[part, rows, :]
            if step >= 2:
                west, east = half(west), half(east)
            store(
                part, pl.ds(RIM + step * RIM, RIM), obj_ref[part, pl.ds(step * RIM, RIM), :],
                gate(west, has_left), gate(east, has_right),
            )


def update_kernel(inner, edge_ref, probe_ref, ext_ref, acc_ref, up, down, left, right, ul, ur, dl, dr, out_ref):
    has_up, has_down = edge_ref[0] != 0, edge_ref[1] != 0
    has_left, has_right = edge_ref[2] != 0, edge_ref[3] != 0
    pr, pi = probe_ref[0], probe_ref[1]
    scale = 1.0 / (jnp.max(pr * pr + pi * pi) + 1e-06)
    lane = lax.broadcasted_iota(jnp.int32, (WIDTH, WIDTH), 1)
    row = lax.broadcasted_iota(jnp.int32, (WIDTH, WIDTH), 0)
    upper, west = row < RIM, lane < RIM

    def gate(value, *conditions):
        for condition in conditions:
            value = jnp.where(condition, value, 0.0)
        return value

    for part in range(2):
        new = {}
        for br in range(3):
            for bc in range(3):
                rows = pl.ds(br * WIDTH, WIDTH)
                total = acc_ref[part, bc, rows, :]
                vert = has_up if br == 0 else has_down
                hori = has_left if bc == 0 else has_right
                if br != 1:
                    total += gate((up if br == 0 else down)[part, bc], vert)
                if bc != 1:
                    total += gate((left if bc == 0 else right)[part, rows, :], hori)
                if br != 1 and bc != 1:
                    diagonal = {(0, 0): ul, (0, 2): ur, (2, 0): dl, (2, 2): dr}[(br, bc)]
                    total += gate(diagonal[part], vert, hori)
                value = ext_ref[part, bc, rows, :] - total * scale
                if not inner:
                    if br != 1:
                        value = jnp.where(jnp.logical_or(vert, (~upper) if br == 0 else upper), value, 0.0)
                    if bc != 1:
                        value = jnp.where(jnp.logical_or(hori, (~west) if bc == 0 else west), value, 0.0)
                    out_ref[part, bc, rows, :] = value
                new[br, bc] = value
        if inner:
            for br in range(3):
                turned = [pltpu.roll(new[br, bc], RIM, 1) for bc in range(3)]
                for half in range(2):
                    full = jnp.where(west, turned[half], turned[half + 1])
                    if br == 0:
                        out_ref[part, pl.ds(0, RIM), pl.ds(half * WIDTH, WIDTH)] = full[RIM:]
                    elif br == 1:
                        out_ref[part, pl.ds(RIM, WIDTH), pl.ds(half * WIDTH, WIDTH)] = full
                    else:
                        out_ref[part, pl.ds(RIM + WIDTH, RIM), pl.ds(half * WIDTH, WIDTH)] = full[:RIM]


def local_call(kernel, out, args, name):
    smem = pl.BlockSpec(memory_space=pltpu.SMEM)
    vmem = pl.BlockSpec(memory_space=pltpu.VMEM)
    return pl.pallas_call(
        kernel,
        out_shape=jax.ShapeDtypeStruct(out, jnp.float32),
        in_specs=[smem] + [vmem] * (len(args) - 1),
        out_specs=vmem,
        compiler_params=pltpu.CompilerParams(vmem_limit_bytes=VMEM_LIMIT),
        name=name,
    )(*args)


def on_device(rows_n, cols_n, obj, probe, amplitudes, centres, members):
    def shift(value, down, right):
        pairs = [
            (r * cols_n + c, (r + down) % rows_n * cols_n + (c + right) % cols_n)
            for r in range(rows_n)
            for c in range(cols_n)
        ]
        return lax.ppermute(value, ("row", "col"), pairs)

    def swap(value, row_bits, col_bits):
        pairs = [
            (r * cols_n + c, (r ^ row_bits) * cols_n + (c ^ col_bits))
            for r in range(rows_n)
            for c in range(cols_n)
        ]
        return lax.ppermute(value, ("row", "col"), pairs)

    tables = [jnp.asarray(table) for table in dft_tables()]
    amp = amplitudes[0, 0]
    rows = centres[0, 0, 0]
    cols = centres[1, 0, 0]
    edge = edges(rows_n, cols_n)
    core = lax.axis_index("col") % 2

    def lanes(strip):
        return jnp.concatenate([strip[:, :WIDTH], strip[:, WIDTH:]], 2)

    corner = lambda r, c: jnp.pad(obj[:, r : r + RIM, c : c + RIM], ((0, 0), (0, 0), (0, RIM)))
    far = TILE - RIM
    ext = local_call(
        assemble_kernel,
        (2, BLOCKS, EXT, WIDTH),
        (
            edge,
            obj,
            shift(obj[:, far:, :], 1, 0),
            shift(obj[:, :RIM, :], -1, 0),
            shift(lanes(obj[:, :, far:]), 0, 1),
            shift(lanes(obj[:, :, :RIM]), 0, -1),
            shift(corner(far, far), 1, 1),
            shift(corner(far, 0), 1, -1),
            shift(corner(0, far), -1, 1),
            shift(corner(0, 0), -1, -1),
        ),
        "assemble",
    )
    iterations = members.shape[0]
    for step in range(iterations):
        last = step == iterations - 1
        acc, sums = patterns(members[step, 0, 0], rows, cols, ext, probe, amp, tables)
        low, high = slice(0, WIDTH), slice(EXT - WIDTH, EXT)
        around = (
            shift(acc[:, :, high], 1, 0),
            shift(acc[:, :, low], -1, 0),
            shift(acc[:, 2], 0, 1),
            shift(acc[:, 0], 0, -1),
            shift(acc[:, 2, high], 1, 1),
            shift(acc[:, 0, high], 1, -1),
            shift(acc[:, 2, low], -1, 1),
            shift(acc[:, 0, low], -1, -1),
        )
        new_ext = local_call(
            functools.partial(update_kernel, last),
            obj.shape if last else ext.shape,
            (edge, probe, ext, acc) + around,
            "update",
        )
        mine = lax.dynamic_slice_in_dim(sums, core * RIM, RIM, 1)
        other = lax.dynamic_slice_in_dim(sums, (1 - core) * RIM, RIM, 1)
        total = mine + swap(other, 0, 1)
        for row_bits, col_bits in ((4, 0), (0, 8), (4, 24), (0, 2), (0, 6), (1, 0), (3, 0)):
            total = total + swap(total, row_bits, col_bits)
        held = lax.dynamic_slice_in_dim(probe, core * RIM, RIM, 1)
        held = held - total[:2] / (total[2] + 1e-06)
        other = swap(held, 0, 1)
        probe = jnp.where(
            core == 0,
            jnp.concatenate([held, other], 1),
            jnp.concatenate([other, held], 1),
        )
        ext = new_ext
    return ext, probe


def solution(mesh):
    in_specs = (
        P(None, "row", "col"),
        P(),
        P("row", "col", None, None, None),
        P(None, "row", "col", None),
        P(None, "row", "col", None),
    )
    out_specs = (P(None, "row", "col"), P())
    body = functools.partial(on_device, mesh.shape["row"], mesh.shape["col"])
    return jax.shard_map(
        body, mesh=mesh, in_specs=in_specs, out_specs=out_specs, check_vma=False
    )
```

```python
import functools
import math

import jax
import jax.numpy as jnp
from jax import lax
from jax.experimental import pallas as pl
from jax.experimental.pallas import tpu as pltpu
from jax.sharding import PartitionSpec as P

WIDTH = 128
RIM = WIDTH // 2
TILE = 256
EXT = TILE + WIDTH
BLOCKS = EXT // WIDTH
GROUP = 4
CHAINS = 2
VMEM_LIMIT = 16 * 1024 * 1024


def split(value):
    high = value.astype(jnp.bfloat16)
    low = (value - high.astype(jnp.float32)).astype(jnp.bfloat16)
    return high, low


def times_right(value, table):
    high, low = split(value)
    return jnp.dot(
        jnp.concatenate([high, low, high], 1), table, preferred_element_type=jnp.float32
    )


def times_left(table, value):
    high, low = split(value)
    return jnp.dot(
        table, jnp.concatenate([high, low, high], 0), preferred_element_type=jnp.float32
    )


def columns_to_rows(value):
    count = value.shape[0] // WIDTH
    parts = [value[i * WIDTH : (i + 1) * WIDTH] for i in range(count)]
    return jnp.concatenate(
        [
            jnp.concatenate([part[:, :WIDTH] for part in parts], 1),
            jnp.concatenate([part[:, WIDTH:] for part in parts], 1),
        ],
        0,
    )


def rows_to_columns(value):
    count = value.shape[1] // WIDTH
    cut = [value[:, i * WIDTH : (i + 1) * WIDTH] for i in range(count)]
    return jnp.concatenate(
        [jnp.concatenate([part[:WIDTH], part[WIDTH:]], 1) for part in cut], 0
    )


def gate(value, *conditions):
    for condition in conditions:
        value = jnp.where(condition, value, 0.0)
    return value


def half_turn(value):
    return pltpu.roll(value, RIM, 1)


def lane_of(rows):
    return lax.broadcasted_iota(jnp.int32, (rows, WIDTH), 1)


def plan_kernel(flags_ref, slots_ref):
    iterations, cap = flags_ref.shape
    for step in range(iterations):

        def note(slot, count):
            live = flags_ref[step, slot] != 0

            @pl.when(live)
            def _():
                slots_ref[step, count] = slot

            return count + live.astype(jnp.int32)

        slots_ref[step, cap] = lax.fori_loop(0, cap, note, jnp.int32(0))


def prepare_kernel(after_ref, amp_ref, probe_ref, ra_ref, lb_ref, la_ref, rb_ref, amp_out, probe_out):
    down = lax.broadcasted_iota(jnp.int32, (WIDTH, WIDTH), 0)
    along = lax.broadcasted_iota(jnp.int32, (WIDTH, WIDTH), 1)
    angle = (down * along % WIDTH).astype(jnp.float32) * (2.0 * math.pi / WIDTH)
    cos_t = jnp.cos(angle) * (1.0 / math.sqrt(WIDTH))
    sin_t = jnp.sin(angle) * (1.0 / math.sqrt(WIDTH))
    cos_h, cos_l = split(cos_t)
    sin_h, sin_l = split(sin_t)
    begin, end = pl.ds(0, WIDTH), pl.ds(WIDTH, WIDTH)
    for place, (cos_p, sin_p) in enumerate(((cos_h, sin_h), (cos_h, sin_h), (cos_l, sin_l))):
        first, second = pl.ds(2 * place * WIDTH, WIDTH), pl.ds((2 * place + 1) * WIDTH, WIDTH)
        for right, left, sign in ((ra_ref, la_ref, 1), (rb_ref, lb_ref, -1)):
            upper, lower = (-sin_p, sin_p) if sign > 0 else (sin_p, -sin_p)
            right[first, begin] = cos_p
            right[first, end] = upper
            right[second, begin] = lower
            right[second, end] = cos_p
            left[begin, first] = cos_p
            left[begin, second] = upper
            left[end, first] = lower
            left[end, second] = cos_p
    amp_out[...] = amp_ref[...]
    probe_out[...] = probe_ref[...]


def pack_kernel(obj_ref, down_ref, up_ref, east_ref, west_ref):
    low = lane_of(WIDTH) < RIM
    up_ref[...] = obj_ref[:, pl.ds(0, RIM), :]
    down_ref[...] = obj_ref[:, pl.ds(TILE - RIM, RIM), :]
    top, bottom = pl.ds(0, WIDTH), pl.ds(WIDTH, WIDTH)
    begin, end = pl.ds(0, WIDTH), pl.ds(TILE - WIDTH, WIDTH)
    for part in range(2):
        west_ref[part] = jnp.where(
            low, obj_ref[part, top, begin], half_turn(obj_ref[part, bottom, begin])
        )
        east_ref[part] = jnp.where(
            low, half_turn(obj_ref[part, top, end]), obj_ref[part, bottom, end]
        )


def corners_kernel(where_ref, up, down, east_ref, west_ref, after_ref):
    after_ref[...] = jnp.zeros_like(after_ref)
    has_up, has_down = where_ref[0] != 0, where_ref[1] != 0
    low = lane_of(RIM) < RIM
    for part in range(2):
        above, below = gate(up[part], has_up), gate(down[part], has_down)
        west_ref[part] = jnp.where(low, above[:, :WIDTH], half_turn(below[:, :WIDTH]))
        east_ref[part] = jnp.where(low, half_turn(above[:, WIDTH:]), below[:, WIDTH:])


def assemble(where_ref, obj_ref, up, down, from_left, from_right, corner_left, corner_right, ext_ref):
    has = [where_ref[i] != 0 for i in range(4)]
    low = lane_of(RIM) < RIM
    for part in range(2):
        for step in range(EXT // RIM):
            rows = pl.ds(step * RIM, RIM)
            if step == 0:
                mid = gate(up[part], has[0])
                left, right = corner_left[part], half_turn(corner_right[part])
            elif step == EXT // RIM - 1:
                mid = gate(down[part], has[1])
                left, right = half_turn(corner_left[part]), corner_right[part]
            else:
                mid = obj_ref[part, pl.ds((step - 1) * RIM, RIM), :]
                at = pl.ds((step - 1) % 2 * RIM, RIM)
                left, right = from_left[part, at, :], from_right[part, at, :]
                if step <= 2:
                    right = half_turn(right)
                else:
                    left = half_turn(left)
            first, second = half_turn(mid[:, :WIDTH]), half_turn(mid[:, WIDTH:])
            ext_ref[part, 0, rows, :] = jnp.where(low, gate(left, has[2]), first)
            ext_ref[part, 1, rows, :] = jnp.where(low, first, second)
            ext_ref[part, 2, rows, :] = jnp.where(low, second, gate(right, has[3]))


def patterns_kernel(first, last, *refs):
    (slots_ref, rows_ref, cols_ref, where_ref), refs = refs[:4], refs[4:]
    cap = rows_ref.shape[0]
    if first:
        (amp_ref, ra_ref, lb_ref, la_ref, rb_ref), halo, refs = refs[:5], refs[5:12], refs[12:]
        probe_ref, refs = refs[0], refs[1:]
        (acc_ref, east_ref, west_ref, mine_ref, other_ref, held_ref, ext_ref, sums_ref) = refs
        assemble(where_ref, *halo, ext_ref)
    else:
        (amp_ref, ra_ref, lb_ref, la_ref, rb_ref), refs = refs[:5], refs[5:]
        (ext_ref, held_mine, held_other), refs = refs[:3], refs[3:]
        (acc_ref, east_ref, west_ref, mine_ref, other_ref, held_ref, probe_ref, sums_ref) = refs
        here = pl.multiple_of(where_ref[4] * RIM, RIM)
        there = pl.multiple_of((1 - where_ref[4]) * RIM, RIM)
        probe_ref[:, pl.ds(here, RIM), :] = held_mine[...]
        probe_ref[:, pl.ds(there, RIM), :] = held_other[...]
    count = slots_ref[cap]
    acc_ref[...] = jnp.zeros_like(acc_ref)
    sums_ref[...] = jnp.zeros_like(sums_ref)
    lane = lane_of(WIDTH)

    def where_is(slot):
        left = cols_ref[slot]
        block = left // WIDTH
        return rows_ref[slot], block, left - block * WIDTH

    def patch(slot):
        top, block, shift = where_is(slot)
        parts = []
        for part in range(2):
            near = ext_ref[part, block, pl.ds(top, WIDTH), :]
            far = ext_ref[part, block + 1, pl.ds(top, WIDTH), :]
            merged = jnp.where(lane >= shift, near, far)
            parts.append(pltpu.roll(merged, (WIDTH - shift) % WIDTH, 1))
        return parts

    def place(slot, update):
        top, block, shift = where_is(slot)
        for part in range(2):
            rolled = pltpu.roll(update[part], shift, 1)
            acc_ref[part, block, pl.ds(top, WIDTH), :] += jnp.where(lane >= shift, rolled, 0.0)
            acc_ref[part, block + 1, pl.ds(top, WIDTH), :] += jnp.where(lane < shift, rolled, 0.0)

    def several(base):
        chosen = [slots_ref[jnp.minimum(base + i, count - 1)] for i in range(GROUP)]
        keep = [(base + i < count).astype(jnp.float32) for i in range(GROUP)]
        pr, pi = probe_ref[0], probe_ref[1]
        waves = []
        objs = []
        for slot in chosen:
            obj_re, obj_im = patch(slot)
            objs.append((obj_re, obj_im))
            waves.append(
                jnp.concatenate([pr * obj_re - pi * obj_im, pr * obj_im + pi * obj_re], 1)
            )
        field = times_right(jnp.concatenate(waves, 0), ra_ref[...])
        field = times_left(lb_ref[...], columns_to_rows(field))
        big_re, big_im = field[:WIDTH], field[WIDTH:]
        inverse = jnp.minimum(lax.rsqrt(big_re * big_re + big_im * big_im), 2.0)
        factor = []
        for which, slot in enumerate(chosen):
            amp = amp_ref[slot].astype(jnp.float32)
            part = inverse[:, which * WIDTH : (which + 1) * WIDTH]
            factor.append((1.0 - amp * part) * keep[which])
        factor = jnp.concatenate(factor, 1)
        chi = jnp.concatenate([big_re * factor, big_im * factor], 0)
        field = times_left(la_ref[...], chi)
        field = times_right(rows_to_columns(field), rb_ref[...])
        grad_re = grad_im = weight = jnp.zeros((WIDTH, WIDTH), jnp.float32)
        for which, slot in enumerate(chosen):
            part = field[which * WIDTH : (which + 1) * WIDTH]
            back_re, back_im = part[:, :WIDTH], part[:, WIDTH:]
            obj_re, obj_im = objs[which]
            place(slot, (pr * back_re + pi * back_im, pr * back_im - pi * back_re))
            grad_re = grad_re + (obj_re * back_re + obj_im * back_im)
            grad_im = grad_im + (obj_re * back_im - obj_im * back_re)
            weight = weight + keep[which] * (obj_re * obj_re + obj_im * obj_im)
        sums_ref[0] += grad_re
        sums_ref[1] += grad_im
        sums_ref[2] += weight

    def chains(index, carry):
        for chain in range(CHAINS):
            several((index * CHAINS + chain) * GROUP)
        return carry

    lax.fori_loop(0, (count + CHAINS * GROUP - 1) // (CHAINS * GROUP), chains, jnp.int32(0))

    here = pl.multiple_of(where_ref[4] * RIM, RIM)
    there = pl.multiple_of((1 - where_ref[4]) * RIM, RIM)
    mine_ref[...] = sums_ref[:, pl.ds(here, RIM), :]
    other_ref[...] = sums_ref[:, pl.ds(there, RIM), :]
    held_ref[...] = probe_ref[:, pl.ds(here, RIM), :]
    if last:
        low = lane_of(EXT // 2) < RIM
        top, bottom = pl.ds(0, EXT // 2), pl.ds(EXT // 2, EXT // 2)
        for part in range(2):
            west_ref[part] = jnp.where(
                low, acc_ref[part, 0, top, :], half_turn(acc_ref[part, 0, bottom, :])
            )
            east_ref[part] = jnp.where(
                low, half_turn(acc_ref[part, 2, top, :]), acc_ref[part, 2, bottom, :]
            )
    else:
        west_ref[...] = acc_ref[:, 0]
        east_ref[...] = acc_ref[:, 2]


def fold_kernel(last, where_ref, acc_in, from_left, from_right, acc_ref, down_ref, up_ref, token_ref):
    token_ref[...] = jnp.zeros_like(token_ref)
    has_left, has_right = where_ref[2] != 0, where_ref[3] != 0
    low = lane_of(EXT // 2) < RIM
    for part in range(2):
        acc_ref[part, 1] = acc_in[part, 1]
        left = gate(from_left[part], has_left)
        right = gate(from_right[part], has_right)
        if last:
            for half in range(2):
                rows = pl.ds(half * (EXT // 2), EXT // 2)
                acc_ref[part, 0, rows, :] = acc_in[part, 0, rows, :] + jnp.where(
                    low, 0.0, left if half else half_turn(left)
                )
                acc_ref[part, 2, rows, :] = acc_in[part, 2, rows, :] + jnp.where(
                    low, half_turn(right) if half else right, 0.0
                )
        else:
            acc_ref[part, 0] = acc_in[part, 0] + left
            acc_ref[part, 2] = acc_in[part, 2] + right
    size = down_ref.shape[2]
    up_ref[...] = acc_ref[:, :, pl.ds(0, size), :]
    down_ref[...] = acc_ref[:, :, pl.ds(EXT - size, size), :]


def peak_scale(probe_ref):
    pr, pi = probe_ref[0], probe_ref[1]
    return 1.0 / (jnp.max(pr * pr + pi * pi) + 1e-06)


def update_kernel(where_ref, probe_ref, ext_ref, acc_ref, up, down, out_ref, token_ref):
    token_ref[...] = jnp.zeros_like(token_ref)
    has = [where_ref[i] != 0 for i in range(4)]
    scale = peak_scale(probe_ref)
    upper = lax.broadcasted_iota(jnp.int32, (WIDTH, WIDTH), 0) < RIM
    west = lane_of(WIDTH) < RIM
    for part in range(2):
        for br in range(3):
            for bc in range(3):
                rows = pl.ds(br * WIDTH, WIDTH)
                total = acc_ref[part, bc, rows, :]
                if br == 0:
                    total = total + gate(up[part, bc], has[0])
                if br == 2:
                    total = total + gate(down[part, bc], has[1])
                value = ext_ref[part, bc, rows, :] - total * scale
                if br != 1:
                    value = gate(value, jnp.logical_or(has[br // 2], (~upper) if br == 0 else upper))
                if bc != 1:
                    value = gate(value, jnp.logical_or(has[2 + bc // 2], (~west) if bc == 0 else west))
                out_ref[part, bc, rows, :] = value


def finish_kernel(where_ref, probe_ref, ext_ref, acc_ref, up, down, out_ref, token_ref):
    token_ref[...] = jnp.zeros_like(token_ref)
    has_up, has_down = where_ref[0] != 0, where_ref[1] != 0
    scale = peak_scale(probe_ref)
    west = lane_of(RIM) < RIM
    for part in range(2):
        for step in range(TILE // RIM):
            rows = pl.ds(RIM + step * RIM, RIM)
            turned = []
            for bc in range(3):
                total = acc_ref[part, bc, rows, :]
                if step == 0:
                    total = total + gate(up[part, bc], has_up)
                if step == TILE // RIM - 1:
                    total = total + gate(down[part, bc], has_down)
                turned.append(half_turn(ext_ref[part, bc, rows, :] - total * scale))
            for half in range(2):
                out_ref[part, pl.ds(step * RIM, RIM), pl.ds(half * WIDTH, WIDTH)] = jnp.where(
                    west, turned[half], turned[half + 1]
                )


def local_call(kernel, name, scalars, arrays, outs, scratch=(), scalar_outs=0):
    smem = pl.BlockSpec(memory_space=pltpu.SMEM)
    vmem = pl.BlockSpec(memory_space=pltpu.VMEM)
    shapes = tuple(
        out if isinstance(out, jax.ShapeDtypeStruct) else jax.ShapeDtypeStruct(out, jnp.float32)
        for out in outs
    )
    return pl.pallas_call(
        kernel,
        out_shape=shapes,
        in_specs=[smem] * len(scalars) + [vmem] * len(arrays),
        out_specs=tuple([smem] * scalar_outs + [vmem] * (len(outs) - scalar_outs)),
        scratch_shapes=list(scratch),
        compiler_params=pltpu.CompilerParams(vmem_limit_bytes=VMEM_LIMIT),
        name=name,
    )(*scalars, *arrays)


def on_device(rows_n, cols_n, obj, probe, amplitudes, centres, members):
    def shift(value, down, right):
        pairs = [
            (r * cols_n + c, (r + down) % rows_n * cols_n + (c + right) % cols_n)
            for r in range(rows_n)
            for c in range(cols_n)
        ]
        return lax.ppermute(value, ("row", "col"), pairs)

    def swap(value, *bits):
        pairs = [
            (r * cols_n + c, (r ^ bits[c % 2][0]) * cols_n + (c ^ bits[c % 2][1]))
            for r in range(rows_n)
            for c in range(cols_n)
        ]
        return lax.ppermute(value, ("row", "col"), pairs)

    x_steps = ((1, 0), (3, 0))
    y_steps = ((0, 2), (0, 6))
    z_steps = ((4, 0), (0, 8), (4, 24))
    ladder = tuple(zip(x_steps + y_steps + z_steps, z_steps + y_steps + x_steps))
    twin = ((0, 1), (0, 1))
    iterations, cap = members.shape[0], members.shape[3]
    rows = centres[0, 0, 0]
    cols = centres[1, 0, 0]
    row, col = lax.axis_index("row"), lax.axis_index("col")
    where = jnp.stack(
        [row > 0, row < rows_n - 1, col > 0, col < cols_n - 1, col % 2 == 1]
    ).astype(jnp.int32)
    ext_shape = (2, BLOCKS, EXT, WIDTH)
    strip = (2, RIM, TILE)
    block = (2, WIDTH, WIDTH)
    corner = (2, RIM, WIDTH)
    to_down, to_up, east, west = local_call(
        pack_kernel, "pack", (), (obj,), (strip, strip, block, block)
    )
    up, down = shift(to_down, 1, 0), shift(to_up, -1, 0)
    from_left, from_right = shift(east, 0, 1), shift(west, 0, -1)
    (slots,) = local_call(
        plan_kernel, "plan", (members[:, 0, 0],), (),
        (jax.ShapeDtypeStruct((iterations, cap + 1), jnp.int32),), scalar_outs=1,
    )
    east, west, after = local_call(
        corners_kernel, "corners", (where,), (up, down), (corner, corner, (8, WIDTH))
    )
    amp = amplitudes[0, 0]
    tall = jax.ShapeDtypeStruct((6 * WIDTH, 2 * WIDTH), jnp.bfloat16)
    wide = jax.ShapeDtypeStruct((2 * WIDTH, 6 * WIDTH), jnp.bfloat16)
    *tables, amp, probe = local_call(
        prepare_kernel, "prepare", (), (after, amp, probe),
        (tall, wide, wide, tall, jax.ShapeDtypeStruct(amp.shape, amp.dtype), block),
    )
    kept = (amp, *tables)
    halo = (obj, up, down, from_left, from_right, shift(east, 0, 1), shift(west, 0, -1))
    halves = None
    ext = None
    sums_scratch = (pltpu.VMEM((3, WIDTH, WIDTH), jnp.float32),)
    for step in range(iterations):
        first, last = step == 0, step == iterations - 1
        size = RIM if last else WIDTH
        strip = (2, EXT // 2, WIDTH) if last else (2, EXT, WIDTH)
        outs = (ext_shape, strip, strip) + ((3, RIM, WIDTH),) * 2 + (corner,)
        kernel = functools.partial(patterns_kernel, first, last)
        scalars = (slots[step], rows, cols, where)
        if first:
            acc, east, west, mine, other, held, ext = local_call(
                kernel, "patterns", scalars, (*kept, *halo, probe), outs + (ext_shape,), sums_scratch
            )
        else:
            acc, east, west, mine, other, held, probe = local_call(
                kernel, "patterns", scalars, (*kept, ext, *halves),
                outs + (block,), sums_scratch,
            )
        from_left = shift(east, 0, 1)
        from_right = shift(west, 0, -1)
        total = mine + swap(other, *twin)
        total = total + swap(total, *ladder[0])
        total = total + swap(total, *ladder[1])
        acc, to_down, to_up, token = local_call(
            functools.partial(fold_kernel, last), "fold", (where,), (acc, from_left, from_right),
            (ext_shape,) + ((2, BLOCKS, size, WIDTH),) * 2 + ((RIM, WIDTH),),
        )
        up = shift(to_down, 1, 0)
        down = shift(to_up, -1, 0)
        total = total + swap(total, *ladder[2]) + token
        total = total + swap(total, *ladder[3])
        total = total + swap(total, *ladder[4])
        total = total + swap(total, *ladder[5])
        ext, token = local_call(
            finish_kernel if last else update_kernel, "finish" if last else "update", (where,),
            (probe, ext, acc, up, down), (obj.shape if last else ext_shape, (RIM, WIDTH)),
        )
        total = total + swap(total, *ladder[6]) + token
        held = held - total[:2] / (total[2] + 1e-06)
        halves = (held, swap(held, *twin))
    held, other = halves
    probe = jnp.where(
        col % 2 == 0, jnp.concatenate([held, other], 1), jnp.concatenate([other, held], 1)
    )
    return ext, probe


def solution(mesh):
    in_specs = (
        P(None, "row", "col"),
        P(),
        P("row", "col", None, None, None),
        P(None, "row", "col", None),
        P(None, "row", "col", None),
    )
    out_specs = (P(None, "row", "col"), P())
    body = functools.partial(on_device, mesh.shape["row"], mesh.shape["col"])
    return jax.shard_map(
        body, mesh=mesh, in_specs=in_specs, out_specs=out_specs, check_vma=False
    )
```

```python
import functools
import math

import jax
import jax.numpy as jnp
from jax import lax
from jax.experimental import pallas as pl
from jax.experimental.pallas import tpu as pltpu
from jax.sharding import PartitionSpec as P

WIDTH = 128
RIM = WIDTH // 2
TILE = 256
EXT = TILE + WIDTH
BLOCKS = EXT // WIDTH
GROUP = 8
CHAINS = 2
VMEM_LIMIT = 16 * 1024 * 1024


def split(value):
    high = value.astype(jnp.bfloat16)
    low = (value - high.astype(jnp.float32)).astype(jnp.bfloat16)
    return high, low


def times_right(value, table):
    high, low = split(value)
    return jnp.dot(
        jnp.concatenate([high, low, high], 1), table, preferred_element_type=jnp.float32
    )


def times_left(table, value):
    high, low = split(value)
    return jnp.dot(
        table, jnp.concatenate([high, low, high], 0), preferred_element_type=jnp.float32
    )


def columns_to_rows(value):
    count = value.shape[0] // WIDTH
    parts = [value[i * WIDTH : (i + 1) * WIDTH] for i in range(count)]
    return jnp.concatenate(
        [
            jnp.concatenate([part[:, :WIDTH] for part in parts], 1),
            jnp.concatenate([part[:, WIDTH:] for part in parts], 1),
        ],
        0,
    )


def rows_to_columns(value):
    count = value.shape[1] // WIDTH
    cut = [value[:, i * WIDTH : (i + 1) * WIDTH] for i in range(count)]
    return jnp.concatenate(
        [jnp.concatenate([part[:WIDTH], part[WIDTH:]], 1) for part in cut], 0
    )


def gate(value, *conditions):
    for condition in conditions:
        value = jnp.where(condition, value, 0.0)
    return value


def half_turn(value):
    return pltpu.roll(value, RIM, 1)


def lane_of(rows):
    return lax.broadcasted_iota(jnp.int32, (rows, WIDTH), 1)


def plan_kernel(flags_ref, slots_ref):
    iterations, cap = flags_ref.shape
    for step in range(iterations):
        count = jnp.int32(0)
        for slot in range(cap):
            slots_ref[step, count] = slot
            count = count + flags_ref[step, slot]
        slots_ref[step, cap] = count


def prepare_kernel(after_ref, amp_ref, probe_ref, ra_ref, lb_ref, la_ref, rb_ref, amp_out, probe_out):
    down = lax.broadcasted_iota(jnp.int32, (WIDTH, WIDTH), 0)
    along = lax.broadcasted_iota(jnp.int32, (WIDTH, WIDTH), 1)
    angle = (down * along % WIDTH).astype(jnp.float32) * (2.0 * math.pi / WIDTH)
    cos_t = jnp.cos(angle) * (1.0 / math.sqrt(WIDTH))
    sin_t = jnp.sin(angle) * (1.0 / math.sqrt(WIDTH))
    cos_h, cos_l = split(cos_t)
    sin_h, sin_l = split(sin_t)
    begin, end = pl.ds(0, WIDTH), pl.ds(WIDTH, WIDTH)
    for place, (cos_p, sin_p) in enumerate(((cos_h, sin_h), (cos_h, sin_h), (cos_l, sin_l))):
        first, second = pl.ds(2 * place * WIDTH, WIDTH), pl.ds((2 * place + 1) * WIDTH, WIDTH)
        for right, left, sign in ((ra_ref, la_ref, 1), (rb_ref, lb_ref, -1)):
            upper, lower = (-sin_p, sin_p) if sign > 0 else (sin_p, -sin_p)
            right[first, begin] = cos_p
            right[first, end] = upper
            right[second, begin] = lower
            right[second, end] = cos_p
            left[begin, first] = cos_p
            left[begin, second] = upper
            left[end, first] = lower
            left[end, second] = cos_p
    amp_out[...] = amp_ref[...]
    probe_out[...] = probe_ref[...]


def pack_kernel(obj_ref, down_ref, up_ref, east_ref, west_ref):
    low = lane_of(WIDTH) < RIM
    up_ref[...] = obj_ref[:, pl.ds(0, RIM), :]
    down_ref[...] = obj_ref[:, pl.ds(TILE - RIM, RIM), :]
    top, bottom = pl.ds(0, WIDTH), pl.ds(WIDTH, WIDTH)
    begin, end = pl.ds(0, WIDTH), pl.ds(TILE - WIDTH, WIDTH)
    for part in range(2):
        west_ref[part] = jnp.where(
            low, obj_ref[part, top, begin], half_turn(obj_ref[part, bottom, begin])
        )
        east_ref[part] = jnp.where(
            low, half_turn(obj_ref[part, top, end]), obj_ref[part, bottom, end]
        )


def corners_kernel(where_ref, up, down, east_ref, west_ref, after_ref):
    after_ref[...] = jnp.zeros_like(after_ref)
    has_up, has_down = where_ref[0] != 0, where_ref[1] != 0
    low = lane_of(RIM) < RIM
    for part in range(2):
        above, below = gate(up[part], has_up), gate(down[part], has_down)
        west_ref[part] = jnp.where(low, above[:, :WIDTH], half_turn(below[:, :WIDTH]))
        east_ref[part] = jnp.where(low, half_turn(above[:, WIDTH:]), below[:, WIDTH:])


def assemble(where_ref, obj_ref, up, down, from_left, from_right, corner_left, corner_right, ext_ref):
    has = [where_ref[i] != 0 for i in range(4)]
    low = lane_of(RIM) < RIM
    for part in range(2):
        for step in range(EXT // RIM):
            rows = pl.ds(step * RIM, RIM)
            if step == 0:
                mid = gate(up[part], has[0])
                left, right = corner_left[part], half_turn(corner_right[part])
            elif step == EXT // RIM - 1:
                mid = gate(down[part], has[1])
                left, right = half_turn(corner_left[part]), corner_right[part]
            else:
                mid = obj_ref[part, pl.ds((step - 1) * RIM, RIM), :]
                at = pl.ds((step - 1) % 2 * RIM, RIM)
                left, right = from_left[part, at, :], from_right[part, at, :]
                if step <= 2:
                    right = half_turn(right)
                else:
                    left = half_turn(left)
            first, second = half_turn(mid[:, :WIDTH]), half_turn(mid[:, WIDTH:])
            ext_ref[part, 0, rows, :] = jnp.where(low, gate(left, has[2]), first)
            ext_ref[part, 1, rows, :] = jnp.where(low, first, second)
            ext_ref[part, 2, rows, :] = jnp.where(low, second, gate(right, has[3]))


def patterns_kernel(step, last, *refs):
    (slots_ref, centres_ref, where_ref), refs = refs[:3], refs[3:]
    first = step == 0
    cap = centres_ref.shape[1]
    if first:
        (amp_ref, ra_ref, lb_ref, la_ref, rb_ref), halo, refs = refs[:5], refs[5:12], refs[12:]
        probe_ref, refs = refs[0], refs[1:]
        (acc_ref, east_ref, west_ref, mine_ref, other_ref, held_ref, ext_ref, sums_ref) = refs
        assemble(where_ref, *halo, ext_ref)
    else:
        (amp_ref, ra_ref, lb_ref, la_ref, rb_ref), refs = refs[:5], refs[5:]
        (ext_ref, held_mine, held_other), refs = refs[:3], refs[3:]
        (acc_ref, east_ref, west_ref, mine_ref, other_ref, held_ref, probe_ref, sums_ref) = refs
        here = pl.multiple_of(where_ref[4] * RIM, RIM)
        there = pl.multiple_of((1 - where_ref[4]) * RIM, RIM)
        probe_ref[:, pl.ds(here, RIM), :] = held_mine[...]
        probe_ref[:, pl.ds(there, RIM), :] = held_other[...]
    count = slots_ref[step, cap]
    acc_ref[...] = jnp.zeros_like(acc_ref)
    sums_ref[...] = jnp.zeros_like(sums_ref)
    lane = lane_of(WIDTH)

    def where_is(slot):
        left = centres_ref[1, slot]
        block = left // WIDTH
        return centres_ref[0, slot], block, left - block * WIDTH

    def patch(slot):
        top, block, shift = where_is(slot)
        parts = []
        for part in range(2):
            near = ext_ref[part, block, pl.ds(top, WIDTH), :]
            far = ext_ref[part, block + 1, pl.ds(top, WIDTH), :]
            merged = jnp.where(lane >= shift, near, far)
            parts.append(pltpu.roll(merged, (WIDTH - shift) % WIDTH, 1))
        return parts

    def place(slot, update):
        top, block, shift = where_is(slot)
        for part in range(2):
            rolled = pltpu.roll(update[part], shift, 1)
            acc_ref[part, block, pl.ds(top, WIDTH), :] += jnp.where(lane >= shift, rolled, 0.0)
            acc_ref[part, block + 1, pl.ds(top, WIDTH), :] += jnp.where(lane < shift, rolled, 0.0)

    def several(base):
        chosen = [slots_ref[step, jnp.minimum(base + i, count - 1)] for i in range(GROUP)]
        keep = [(base + i < count).astype(jnp.float32) for i in range(GROUP)]
        pr, pi = probe_ref[0], probe_ref[1]
        waves = []
        objs = []
        for slot in chosen:
            obj_re, obj_im = patch(slot)
            objs.append((obj_re, obj_im))
            waves.append(
                jnp.concatenate([pr * obj_re - pi * obj_im, pr * obj_im + pi * obj_re], 1)
            )
        field = times_right(jnp.concatenate(waves, 0), ra_ref[...])
        field = times_left(lb_ref[...], columns_to_rows(field))
        big_re, big_im = field[:WIDTH], field[WIDTH:]
        inverse = jnp.minimum(lax.rsqrt(big_re * big_re + big_im * big_im), 2.0)
        factor = []
        for which, slot in enumerate(chosen):
            amp = amp_ref[slot].astype(jnp.float32)
            part = inverse[:, which * WIDTH : (which + 1) * WIDTH]
            factor.append((1.0 - amp * part) * keep[which])
        factor = jnp.concatenate(factor, 1)
        chi = jnp.concatenate([big_re * factor, big_im * factor], 0)
        field = times_left(la_ref[...], chi)
        field = times_right(rows_to_columns(field), rb_ref[...])
        grad_re = grad_im = weight = jnp.zeros((WIDTH, WIDTH), jnp.float32)
        for which, slot in enumerate(chosen):
            part = field[which * WIDTH : (which + 1) * WIDTH]
            back_re, back_im = part[:, :WIDTH], part[:, WIDTH:]
            obj_re, obj_im = objs[which]
            place(slot, (pr * back_re + pi * back_im, pr * back_im - pi * back_re))
            grad_re = grad_re + (obj_re * back_re + obj_im * back_im)
            grad_im = grad_im + (obj_re * back_im - obj_im * back_re)
            weight = weight + keep[which] * (obj_re * obj_re + obj_im * obj_im)
        sums_ref[0] += grad_re
        sums_ref[1] += grad_im
        sums_ref[2] += weight

    def chains(index, carry):
        for chain in range(CHAINS):
            several((index * CHAINS + chain) * GROUP)
        return carry

    lax.fori_loop(0, (count + CHAINS * GROUP - 1) // (CHAINS * GROUP), chains, jnp.int32(0))

    here = pl.multiple_of(where_ref[4] * RIM, RIM)
    there = pl.multiple_of((1 - where_ref[4]) * RIM, RIM)
    mine_ref[...] = sums_ref[:, pl.ds(here, RIM), :]
    other_ref[...] = sums_ref[:, pl.ds(there, RIM), :]
    held_ref[...] = probe_ref[:, pl.ds(here, RIM), :]
    if last:
        low = lane_of(EXT // 2) < RIM
        top, bottom = pl.ds(0, EXT // 2), pl.ds(EXT // 2, EXT // 2)
        for part in range(2):
            west_ref[part] = jnp.where(
                low, acc_ref[part, 0, top, :], half_turn(acc_ref[part, 0, bottom, :])
            )
            east_ref[part] = jnp.where(
                low, half_turn(acc_ref[part, 2, top, :]), acc_ref[part, 2, bottom, :]
            )
    else:
        west_ref[...] = acc_ref[:, 0]
        east_ref[...] = acc_ref[:, 2]


def fold_kernel(last, where_ref, acc_in, from_left, from_right, acc_ref, down_ref, up_ref, token_ref):
    token_ref[...] = jnp.zeros_like(token_ref)
    has_left, has_right = where_ref[2] != 0, where_ref[3] != 0
    low = lane_of(EXT // 2) < RIM
    for part in range(2):
        acc_ref[part, 1] = acc_in[part, 1]
        left = gate(from_left[part], has_left)
        right = gate(from_right[part], has_right)
        if last:
            for half in range(2):
                rows = pl.ds(half * (EXT // 2), EXT // 2)
                acc_ref[part, 0, rows, :] = acc_in[part, 0, rows, :] + jnp.where(
                    low, 0.0, left if half else half_turn(left)
                )
                acc_ref[part, 2, rows, :] = acc_in[part, 2, rows, :] + jnp.where(
                    low, half_turn(right) if half else right, 0.0
                )
        else:
            acc_ref[part, 0] = acc_in[part, 0] + left
            acc_ref[part, 2] = acc_in[part, 2] + right
    size = down_ref.shape[2]
    up_ref[...] = acc_ref[:, :, pl.ds(0, size), :]
    down_ref[...] = acc_ref[:, :, pl.ds(EXT - size, size), :]


def peak_scale(probe_ref):
    pr, pi = probe_ref[0], probe_ref[1]
    return 1.0 / (jnp.max(pr * pr + pi * pi) + 1e-06)


def update_kernel(where_ref, probe_ref, ext_ref, acc_ref, up, down, out_ref, token_ref):
    token_ref[...] = jnp.zeros_like(token_ref)
    has = [where_ref[i] != 0 for i in range(4)]
    scale = peak_scale(probe_ref)
    upper = lax.broadcasted_iota(jnp.int32, (WIDTH, WIDTH), 0) < RIM
    west = lane_of(WIDTH) < RIM
    for part in range(2):
        for br in range(3):
            for bc in range(3):
                rows = pl.ds(br * WIDTH, WIDTH)
                total = acc_ref[part, bc, rows, :]
                if br == 0:
                    total = total + gate(up[part, bc], has[0])
                if br == 2:
                    total = total + gate(down[part, bc], has[1])
                value = ext_ref[part, bc, rows, :] - total * scale
                if br != 1:
                    value = gate(value, jnp.logical_or(has[br // 2], (~upper) if br == 0 else upper))
                if bc != 1:
                    value = gate(value, jnp.logical_or(has[2 + bc // 2], (~west) if bc == 0 else west))
                out_ref[part, bc, rows, :] = value


def finish_kernel(where_ref, probe_ref, ext_ref, acc_ref, up, down, out_ref, token_ref):
    token_ref[...] = jnp.zeros_like(token_ref)
    has_up, has_down = where_ref[0] != 0, where_ref[1] != 0
    scale = peak_scale(probe_ref)
    west = lane_of(RIM) < RIM
    for part in range(2):
        for step in range(TILE // RIM):
            rows = pl.ds(RIM + step * RIM, RIM)
            turned = []
            for bc in range(3):
                total = acc_ref[part, bc, rows, :]
                if step == 0:
                    total = total + gate(up[part, bc], has_up)
                if step == TILE // RIM - 1:
                    total = total + gate(down[part, bc], has_down)
                turned.append(half_turn(ext_ref[part, bc, rows, :] - total * scale))
            for half in range(2):
                out_ref[part, pl.ds(step * RIM, RIM), pl.ds(half * WIDTH, WIDTH)] = jnp.where(
                    west, turned[half], turned[half + 1]
                )


def local_call(kernel, name, scalars, arrays, outs, scratch=(), scalar_outs=0):
    smem = pl.BlockSpec(memory_space=pltpu.SMEM)
    vmem = pl.BlockSpec(memory_space=pltpu.VMEM)
    shapes = tuple(
        out if isinstance(out, jax.ShapeDtypeStruct) else jax.ShapeDtypeStruct(out, jnp.float32)
        for out in outs
    )
    return pl.pallas_call(
        kernel,
        out_shape=shapes,
        in_specs=[smem] * len(scalars) + [vmem] * len(arrays),
        out_specs=tuple([smem] * scalar_outs + [vmem] * (len(outs) - scalar_outs)),
        scratch_shapes=list(scratch),
        compiler_params=pltpu.CompilerParams(vmem_limit_bytes=VMEM_LIMIT),
        name=name,
    )(*scalars, *arrays)


def on_device(rows_n, cols_n, obj, probe, amplitudes, centres, members):
    def shift(value, down, right):
        pairs = [
            (r * cols_n + c, (r + down) % rows_n * cols_n + (c + right) % cols_n)
            for r in range(rows_n)
            for c in range(cols_n)
        ]
        return lax.ppermute(value, ("row", "col"), pairs)

    def swap(value, *bits):
        pairs = [
            (r * cols_n + c, (r ^ bits[c % 2][0]) * cols_n + (c ^ bits[c % 2][1]))
            for r in range(rows_n)
            for c in range(cols_n)
        ]
        return lax.ppermute(value, ("row", "col"), pairs)

    x_steps = ((1, 0), (2, 0), (3, 0))
    y_steps = ((0, 2), (0, 4), (0, 6))
    z_steps = ((4, 0), (0, 8), (4, 8))
    z_far = (4, 24)

    def four(value, steps):
        one, two, three = (swap(value, *bits) for bits in steps)
        return (value + one) + (two + three)

    twin = ((0, 1), (0, 1))
    iterations, cap = members.shape[0], members.shape[3]
    places = centres[:, 0, 0]
    row, col = lax.axis_index("row"), lax.axis_index("col")
    where = jnp.stack(
        [row > 0, row < rows_n - 1, col > 0, col < cols_n - 1, col % 2 == 1]
    ).astype(jnp.int32)
    ext_shape = (2, BLOCKS, EXT, WIDTH)
    strip = (2, RIM, TILE)
    block = (2, WIDTH, WIDTH)
    corner = (2, RIM, WIDTH)
    to_down, to_up, east, west = local_call(
        pack_kernel, "pack", (), (obj,), (strip, strip, block, block)
    )
    up, down = shift(to_down, 1, 0), shift(to_up, -1, 0)
    from_left, from_right = shift(east, 0, 1), shift(west, 0, -1)
    (slots,) = local_call(
        plan_kernel, "plan", (members[:, 0, 0],), (),
        (jax.ShapeDtypeStruct((iterations, cap + 1), jnp.int32),), scalar_outs=1,
    )
    east, west, after = local_call(
        corners_kernel, "corners", (where,), (up, down), (corner, corner, (8, WIDTH))
    )
    amp = amplitudes[0, 0]
    tall = jax.ShapeDtypeStruct((6 * WIDTH, 2 * WIDTH), jnp.bfloat16)
    wide = jax.ShapeDtypeStruct((2 * WIDTH, 6 * WIDTH), jnp.bfloat16)
    *tables, amp, probe = local_call(
        prepare_kernel, "prepare", (), (after, amp, probe),
        (tall, wide, wide, tall, jax.ShapeDtypeStruct(amp.shape, amp.dtype), block),
    )
    kept = (amp, *tables)
    halo = (obj, up, down, from_left, from_right, shift(east, 0, 1), shift(west, 0, -1))
    halves = None
    ext = None
    sums_scratch = (pltpu.VMEM((3, WIDTH, WIDTH), jnp.float32),)
    for step in range(iterations):
        first, last = step == 0, step == iterations - 1
        size = RIM if last else WIDTH
        strip = (2, EXT // 2, WIDTH) if last else (2, EXT, WIDTH)
        outs = (ext_shape, strip, strip) + ((3, RIM, WIDTH),) * 2 + (corner,)
        kernel = functools.partial(patterns_kernel, step, last)
        scalars = (slots, places, where)
        if first:
            acc, east, west, mine, other, held, ext = local_call(
                kernel, "patterns", scalars, (*kept, *halo, probe), outs + (ext_shape,), sums_scratch
            )
        else:
            acc, east, west, mine, other, held, probe = local_call(
                kernel, "patterns", scalars, (*kept, ext, *halves),
                outs + (block,), sums_scratch,
            )
        from_left = shift(east, 0, 1)
        from_right = shift(west, 0, -1)
        total = mine + swap(other, *twin)
        total = four(total, tuple(zip(x_steps, y_steps)))
        acc, to_down, to_up, token = local_call(
            functools.partial(fold_kernel, last), "fold", (where,), (acc, from_left, from_right),
            (ext_shape,) + ((2, BLOCKS, size, WIDTH),) * 2 + ((RIM, WIDTH),),
        )
        up = shift(to_down, 1, 0)
        down = shift(to_up, -1, 0)
        total = four(total, tuple(zip(y_steps, x_steps))) + token
        total = four(total, tuple(zip(z_steps, z_steps)))
        ext, token = local_call(
            finish_kernel if last else update_kernel, "finish" if last else "update", (where,),
            (probe, ext, acc, up, down), (obj.shape if last else ext_shape, (RIM, WIDTH)),
        )
        total = total + swap(total, z_far, z_far) + token
        held = held - total[:2] / (total[2] + 1e-06)
        halves = (held, swap(held, *twin))
    held, other = halves
    probe = jnp.where(
        col % 2 == 0, jnp.concatenate([held, other], 1), jnp.concatenate([other, held], 1)
    )
    return ext, probe


def solution(mesh):
    in_specs = (
        P(None, "row", "col"),
        P(),
        P("row", "col", None, None, None),
        P(None, "row", "col", None),
        P(None, "row", "col", None),
    )
    out_specs = (P(None, "row", "col"), P())
    body = functools.partial(on_device, mesh.shape["row"], mesh.shape["col"])
    return jax.shard_map(
        body, mesh=mesh, in_specs=in_specs, out_specs=out_specs, check_vma=False
    )
```

```python
import functools
import math

import jax
import jax.numpy as jnp
from jax import lax
from jax.experimental import pallas as pl
from jax.experimental.pallas import tpu as pltpu
from jax.sharding import PartitionSpec as P

WIDTH = 128
RIM = WIDTH // 2
TILE = 256
EXT = TILE + WIDTH
BLOCKS = EXT // WIDTH
GROUP = 8
CHAINS = 2
VMEM_LIMIT = 16 * 1024 * 1024


def split(value):
    high = value.astype(jnp.bfloat16)
    low = (value - high.astype(jnp.float32)).astype(jnp.bfloat16)
    return high, low


def times_right(value, table):
    high, low = split(value)
    return jnp.dot(
        jnp.concatenate([high, low, high], 1), table, preferred_element_type=jnp.float32
    )


def times_left(table, value):
    high, low = split(value)
    return jnp.dot(
        table, jnp.concatenate([high, low, high], 0), preferred_element_type=jnp.float32
    )


def columns_to_rows(value):
    count = value.shape[0] // WIDTH
    parts = [value[i * WIDTH : (i + 1) * WIDTH] for i in range(count)]
    return jnp.concatenate(
        [
            jnp.concatenate([part[:, :WIDTH] for part in parts], 1),
            jnp.concatenate([part[:, WIDTH:] for part in parts], 1),
        ],
        0,
    )


def rows_to_columns(value):
    count = value.shape[1] // WIDTH
    cut = [value[:, i * WIDTH : (i + 1) * WIDTH] for i in range(count)]
    return jnp.concatenate(
        [jnp.concatenate([part[:WIDTH], part[WIDTH:]], 1) for part in cut], 0
    )


def gate(value, *conditions):
    for condition in conditions:
        value = jnp.where(condition, value, 0.0)
    return value


def half_turn(value):
    return pltpu.roll(value, RIM, 1)


def lane_of(rows):
    return lax.broadcasted_iota(jnp.int32, (rows, WIDTH), 1)


def plan_kernel(flags_ref, slots_ref):
    iterations, cap = flags_ref.shape
    for step in range(iterations):
        count = jnp.int32(0)
        for slot in range(cap):
            slots_ref[step, count] = slot
            count = count + flags_ref[step, slot]
        slots_ref[step, cap] = count


def prepare_kernel(after_ref, amp_ref, probe_ref, ra_ref, lb_ref, la_ref, rb_ref, amp_out, probe_out):
    down = lax.broadcasted_iota(jnp.int32, (WIDTH, WIDTH), 0)
    along = lax.broadcasted_iota(jnp.int32, (WIDTH, WIDTH), 1)
    angle = (down * along % WIDTH).astype(jnp.float32) * (2.0 * math.pi / WIDTH)
    cos_t = jnp.cos(angle) * (1.0 / math.sqrt(WIDTH))
    sin_t = jnp.sin(angle) * (1.0 / math.sqrt(WIDTH))
    cos_h, cos_l = split(cos_t)
    sin_h, sin_l = split(sin_t)
    begin, end = pl.ds(0, WIDTH), pl.ds(WIDTH, WIDTH)
    for place, (cos_p, sin_p) in enumerate(((cos_h, sin_h), (cos_h, sin_h), (cos_l, sin_l))):
        first, second = pl.ds(2 * place * WIDTH, WIDTH), pl.ds((2 * place + 1) * WIDTH, WIDTH)
        for right, left, sign in ((ra_ref, la_ref, 1), (rb_ref, lb_ref, -1)):
            upper, lower = (-sin_p, sin_p) if sign > 0 else (sin_p, -sin_p)
            right[first, begin] = cos_p
            right[first, end] = upper
            right[second, begin] = lower
            right[second, end] = cos_p
            left[begin, first] = cos_p
            left[begin, second] = upper
            left[end, first] = lower
            left[end, second] = cos_p
    amp_out[...] = amp_ref[...]
    probe_out[...] = probe_ref[...]


def pack_kernel(obj_ref, down_ref, up_ref, east_ref, west_ref):
    low = lane_of(WIDTH) < RIM
    up_ref[...] = obj_ref[:, pl.ds(0, RIM), :]
    down_ref[...] = obj_ref[:, pl.ds(TILE - RIM, RIM), :]
    top, bottom = pl.ds(0, WIDTH), pl.ds(WIDTH, WIDTH)
    begin, end = pl.ds(0, WIDTH), pl.ds(TILE - WIDTH, WIDTH)
    for part in range(2):
        west_ref[part] = jnp.where(
            low, obj_ref[part, top, begin], half_turn(obj_ref[part, bottom, begin])
        )
        east_ref[part] = jnp.where(
            low, half_turn(obj_ref[part, top, end]), obj_ref[part, bottom, end]
        )


def corners_kernel(where_ref, up, down, east_ref, west_ref, after_ref):
    after_ref[...] = jnp.zeros_like(after_ref)
    has_up, has_down = where_ref[0] != 0, where_ref[1] != 0
    low = lane_of(RIM) < RIM
    for part in range(2):
        above, below = gate(up[part], has_up), gate(down[part], has_down)
        west_ref[part] = jnp.where(low, above[:, :WIDTH], half_turn(below[:, :WIDTH]))
        east_ref[part] = jnp.where(low, half_turn(above[:, WIDTH:]), below[:, WIDTH:])


def assemble(where_ref, obj_ref, up, down, from_left, from_right, corner_left, corner_right, ext_ref):
    has = [where_ref[i] != 0 for i in range(4)]
    low = lane_of(RIM) < RIM
    for part in range(2):
        for step in range(EXT // RIM):
            rows = pl.ds(step * RIM, RIM)
            if step == 0:
                mid = gate(up[part], has[0])
                left, right = corner_left[part], half_turn(corner_right[part])
            elif step == EXT // RIM - 1:
                mid = gate(down[part], has[1])
                left, right = half_turn(corner_left[part]), corner_right[part]
            else:
                mid = obj_ref[part, pl.ds((step - 1) * RIM, RIM), :]
                at = pl.ds((step - 1) % 2 * RIM, RIM)
                left, right = from_left[part, at, :], from_right[part, at, :]
                if step <= 2:
                    right = half_turn(right)
                else:
                    left = half_turn(left)
            first, second = half_turn(mid[:, :WIDTH]), half_turn(mid[:, WIDTH:])
            ext_ref[part, 0, rows, :] = jnp.where(low, gate(left, has[2]), first)
            ext_ref[part, 1, rows, :] = jnp.where(low, first, second)
            ext_ref[part, 2, rows, :] = jnp.where(low, second, gate(right, has[3]))


def patterns_kernel(step, last, *refs):
    (slots_ref, centres_ref, where_ref), refs = refs[:3], refs[3:]
    first = step == 0
    cap = centres_ref.shape[1]
    if first:
        (amp_ref, ra_ref, lb_ref, la_ref, rb_ref), halo, refs = refs[:5], refs[5:12], refs[12:]
        probe_ref, refs = refs[0], refs[1:]
        (acc_ref, east_ref, west_ref, mine_ref, other_ref, held_ref, spare_ref, ext_ref, sums_ref) = refs
        assemble(where_ref, *halo, ext_ref)
    else:
        (amp_ref, ra_ref, lb_ref, la_ref, rb_ref), refs = refs[:5], refs[5:]
        (ext_ref, held_mine, held_other), refs = refs[:3], refs[3:]
        (acc_ref, east_ref, west_ref, mine_ref, other_ref, held_ref, spare_ref, probe_ref, sums_ref) = refs
        here = pl.multiple_of(where_ref[4] * RIM, RIM)
        there = pl.multiple_of((1 - where_ref[4]) * RIM, RIM)
        probe_ref[:, pl.ds(here, RIM), :] = held_mine[...]
        probe_ref[:, pl.ds(there, RIM), :] = held_other[...]
    count = slots_ref[step, cap]
    acc_ref[...] = jnp.zeros_like(acc_ref)
    sums_ref[...] = jnp.zeros_like(sums_ref)
    lane = lane_of(WIDTH)

    def where_is(slot):
        left = centres_ref[1, slot]
        block = left // WIDTH
        return centres_ref[0, slot], block, left - block * WIDTH

    def patch(slot):
        top, block, shift = where_is(slot)
        parts = []
        for part in range(2):
            near = ext_ref[part, block, pl.ds(top, WIDTH), :]
            far = ext_ref[part, block + 1, pl.ds(top, WIDTH), :]
            merged = jnp.where(lane >= shift, near, far)
            parts.append(pltpu.roll(merged, (WIDTH - shift) % WIDTH, 1))
        return parts

    def place(slot, update):
        top, block, shift = where_is(slot)
        for part in range(2):
            rolled = pltpu.roll(update[part], shift, 1)
            acc_ref[part, block, pl.ds(top, WIDTH), :] += jnp.where(lane >= shift, rolled, 0.0)
            acc_ref[part, block + 1, pl.ds(top, WIDTH), :] += jnp.where(lane < shift, rolled, 0.0)

    def several(base):
        chosen = [slots_ref[step, jnp.minimum(base + i, count - 1)] for i in range(GROUP)]
        keep = [(base + i < count).astype(jnp.float32) for i in range(GROUP)]
        pr, pi = probe_ref[0], probe_ref[1]
        waves = []
        objs = []
        for slot in chosen:
            obj_re, obj_im = patch(slot)
            objs.append((obj_re, obj_im))
            waves.append(
                jnp.concatenate([pr * obj_re - pi * obj_im, pr * obj_im + pi * obj_re], 1)
            )
        field = times_right(jnp.concatenate(waves, 0), ra_ref[...])
        field = times_left(lb_ref[...], columns_to_rows(field))
        big_re, big_im = field[:WIDTH], field[WIDTH:]
        inverse = jnp.minimum(lax.rsqrt(big_re * big_re + big_im * big_im), 2.0)
        factor = []
        for which, slot in enumerate(chosen):
            amp = amp_ref[slot].astype(jnp.float32)
            part = inverse[:, which * WIDTH : (which + 1) * WIDTH]
            factor.append((1.0 - amp * part) * keep[which])
        factor = jnp.concatenate(factor, 1)
        chi = jnp.concatenate([big_re * factor, big_im * factor], 0)
        field = times_left(la_ref[...], chi)
        field = times_right(rows_to_columns(field), rb_ref[...])
        grad_re = grad_im = weight = jnp.zeros((WIDTH, WIDTH), jnp.float32)
        for which, slot in enumerate(chosen):
            part = field[which * WIDTH : (which + 1) * WIDTH]
            back_re, back_im = part[:, :WIDTH], part[:, WIDTH:]
            obj_re, obj_im = objs[which]
            place(slot, (pr * back_re + pi * back_im, pr * back_im - pi * back_re))
            grad_re = grad_re + (obj_re * back_re + obj_im * back_im)
            grad_im = grad_im + (obj_re * back_im - obj_im * back_re)
            weight = weight + keep[which] * (obj_re * obj_re + obj_im * obj_im)
        sums_ref[0] += grad_re
        sums_ref[1] += grad_im
        sums_ref[2] += weight

    def chains(index, carry):
        for chain in range(CHAINS):
            several((index * CHAINS + chain) * GROUP)
        return carry

    lax.fori_loop(0, (count + CHAINS * GROUP - 1) // (CHAINS * GROUP), chains, jnp.int32(0))

    here = pl.multiple_of(where_ref[4] * RIM, RIM)
    there = pl.multiple_of((1 - where_ref[4]) * RIM, RIM)
    mine_ref[...] = sums_ref[:, pl.ds(here, RIM), :]
    other_ref[...] = sums_ref[:, pl.ds(there, RIM), :]
    held_ref[...] = probe_ref[:, pl.ds(here, RIM), :]
    spare_ref[...] = probe_ref[:, pl.ds(there, RIM), :]
    if last:
        low = lane_of(EXT // 2) < RIM
        top, bottom = pl.ds(0, EXT // 2), pl.ds(EXT // 2, EXT // 2)
        for part in range(2):
            west_ref[part] = jnp.where(
                low, acc_ref[part, 0, top, :], half_turn(acc_ref[part, 0, bottom, :])
            )
            east_ref[part] = jnp.where(
                low, half_turn(acc_ref[part, 2, top, :]), acc_ref[part, 2, bottom, :]
            )
    else:
        west_ref[...] = acc_ref[:, 0]
        east_ref[...] = acc_ref[:, 2]


def fold_kernel(last, where_ref, acc_in, from_left, from_right, acc_ref, down_ref, up_ref, token_ref):
    token_ref[...] = jnp.zeros_like(token_ref)
    has_left, has_right = where_ref[2] != 0, where_ref[3] != 0
    low = lane_of(EXT // 2) < RIM
    for part in range(2):
        acc_ref[part, 1] = acc_in[part, 1]
        left = gate(from_left[part], has_left)
        right = gate(from_right[part], has_right)
        if last:
            for half in range(2):
                rows = pl.ds(half * (EXT // 2), EXT // 2)
                acc_ref[part, 0, rows, :] = acc_in[part, 0, rows, :] + jnp.where(
                    low, 0.0, left if half else half_turn(left)
                )
                acc_ref[part, 2, rows, :] = acc_in[part, 2, rows, :] + jnp.where(
                    low, half_turn(right) if half else right, 0.0
                )
        else:
            acc_ref[part, 0] = acc_in[part, 0] + left
            acc_ref[part, 2] = acc_in[part, 2] + right
    size = down_ref.shape[2]
    up_ref[...] = acc_ref[:, :, pl.ds(0, size), :]
    down_ref[...] = acc_ref[:, :, pl.ds(EXT - size, size), :]


def peak_scale(probe_ref):
    pr, pi = probe_ref[0], probe_ref[1]
    return 1.0 / (jnp.max(pr * pr + pi * pi) + 1e-06)


def update_kernel(where_ref, probe_ref, ext_ref, acc_ref, up, down, out_ref, token_ref):
    token_ref[...] = jnp.zeros_like(token_ref)
    has = [where_ref[i] != 0 for i in range(4)]
    scale = peak_scale(probe_ref)
    upper = lax.broadcasted_iota(jnp.int32, (WIDTH, WIDTH), 0) < RIM
    west = lane_of(WIDTH) < RIM
    for part in range(2):
        for br in range(3):
            for bc in range(3):
                rows = pl.ds(br * WIDTH, WIDTH)
                total = acc_ref[part, bc, rows, :]
                if br == 0:
                    total = total + gate(up[part, bc], has[0])
                if br == 2:
                    total = total + gate(down[part, bc], has[1])
                value = ext_ref[part, bc, rows, :] - total * scale
                if br != 1:
                    value = gate(value, jnp.logical_or(has[br // 2], (~upper) if br == 0 else upper))
                if bc != 1:
                    value = gate(value, jnp.logical_or(has[2 + bc // 2], (~west) if bc == 0 else west))
                out_ref[part, bc, rows, :] = value


def finish_kernel(where_ref, probe_ref, ext_ref, acc_ref, up, down, out_ref, token_ref):
    token_ref[...] = jnp.zeros_like(token_ref)
    has_up, has_down = where_ref[0] != 0, where_ref[1] != 0
    scale = peak_scale(probe_ref)
    west = lane_of(RIM) < RIM
    for part in range(2):
        for step in range(TILE // RIM):
            rows = pl.ds(RIM + step * RIM, RIM)
            turned = []
            for bc in range(3):
                total = acc_ref[part, bc, rows, :]
                if step == 0:
                    total = total + gate(up[part, bc], has_up)
                if step == TILE // RIM - 1:
                    total = total + gate(down[part, bc], has_down)
                turned.append(half_turn(ext_ref[part, bc, rows, :] - total * scale))
            for half in range(2):
                out_ref[part, pl.ds(step * RIM, RIM), pl.ds(half * WIDTH, WIDTH)] = jnp.where(
                    west, turned[half], turned[half + 1]
                )


def local_call(kernel, name, scalars, arrays, outs, scratch=(), scalar_outs=0):
    smem = pl.BlockSpec(memory_space=pltpu.SMEM)
    vmem = pl.BlockSpec(memory_space=pltpu.VMEM)
    shapes = tuple(
        out if isinstance(out, jax.ShapeDtypeStruct) else jax.ShapeDtypeStruct(out, jnp.float32)
        for out in outs
    )
    return pl.pallas_call(
        kernel,
        out_shape=shapes,
        in_specs=[smem] * len(scalars) + [vmem] * len(arrays),
        out_specs=tuple([smem] * scalar_outs + [vmem] * (len(outs) - scalar_outs)),
        scratch_shapes=list(scratch),
        compiler_params=pltpu.CompilerParams(vmem_limit_bytes=VMEM_LIMIT),
        name=name,
    )(*scalars, *arrays)


def on_device(rows_n, cols_n, obj, probe, amplitudes, centres, members):
    def shift(value, down, right):
        pairs = [
            (r * cols_n + c, (r + down) % rows_n * cols_n + (c + right) % cols_n)
            for r in range(rows_n)
            for c in range(cols_n)
        ]
        return lax.ppermute(value, ("row", "col"), pairs)

    def swap(value, *bits):
        pairs = [
            (r * cols_n + c, (r ^ bits[c % 2][0]) * cols_n + (c ^ bits[c % 2][1]))
            for r in range(rows_n)
            for c in range(cols_n)
        ]
        return lax.ppermute(value, ("row", "col"), pairs)

    x_steps = ((1, 0), (2, 0), (3, 0))
    y_steps = ((0, 2), (0, 4), (0, 6))
    z_steps = ((4, 0), (0, 8), (4, 8))
    z_far = (4, 24)
    z_twin = (4, 25)

    def four(value, steps):
        one, two, three = (swap(value, *bits) for bits in steps)
        return (value + one) + (two + three)

    twin = ((0, 1), (0, 1))
    iterations, cap = members.shape[0], members.shape[3]
    places = centres[:, 0, 0]
    row, col = lax.axis_index("row"), lax.axis_index("col")
    where = jnp.stack(
        [row > 0, row < rows_n - 1, col > 0, col < cols_n - 1, col % 2 == 1]
    ).astype(jnp.int32)
    ext_shape = (2, BLOCKS, EXT, WIDTH)
    strip = (2, RIM, TILE)
    block = (2, WIDTH, WIDTH)
    corner = (2, RIM, WIDTH)
    to_down, to_up, east, west = local_call(
        pack_kernel, "pack", (), (obj,), (strip, strip, block, block)
    )
    up, down = shift(to_down, 1, 0), shift(to_up, -1, 0)
    from_left, from_right = shift(east, 0, 1), shift(west, 0, -1)
    (slots,) = local_call(
        plan_kernel, "plan", (members[:, 0, 0],), (),
        (jax.ShapeDtypeStruct((iterations, cap + 1), jnp.int32),), scalar_outs=1,
    )
    east, west, after = local_call(
        corners_kernel, "corners", (where,), (up, down), (corner, corner, (8, WIDTH))
    )
    amp = amplitudes[0, 0]
    tall = jax.ShapeDtypeStruct((6 * WIDTH, 2 * WIDTH), jnp.bfloat16)
    wide = jax.ShapeDtypeStruct((2 * WIDTH, 6 * WIDTH), jnp.bfloat16)
    *tables, amp, probe = local_call(
        prepare_kernel, "prepare", (), (after, amp, probe),
        (tall, wide, wide, tall, jax.ShapeDtypeStruct(amp.shape, amp.dtype), block),
    )
    kept = (amp, *tables)
    halo = (obj, up, down, from_left, from_right, shift(east, 0, 1), shift(west, 0, -1))
    halves = None
    ext = None
    sums_scratch = (pltpu.VMEM((3, WIDTH, WIDTH), jnp.float32),)
    for step in range(iterations):
        first, last = step == 0, step == iterations - 1
        size = RIM if last else WIDTH
        strip = (2, EXT // 2, WIDTH) if last else (2, EXT, WIDTH)
        outs = (ext_shape, strip, strip) + ((3, RIM, WIDTH),) * 2 + (corner,) * 2
        kernel = functools.partial(patterns_kernel, step, last)
        scalars = (slots, places, where)
        if first:
            acc, east, west, mine, other, held, spare, ext = local_call(
                kernel, "patterns", scalars, (*kept, *halo, probe), outs + (ext_shape,), sums_scratch
            )
        else:
            acc, east, west, mine, other, held, spare, probe = local_call(
                kernel, "patterns", scalars, (*kept, ext, *halves),
                outs + (block,), sums_scratch,
            )
        from_left = shift(east, 0, 1)
        from_right = shift(west, 0, -1)
        total = mine + swap(other, *twin)
        total = four(total, tuple(zip(x_steps, z_steps)))
        acc, to_down, to_up, token = local_call(
            functools.partial(fold_kernel, last), "fold", (where,), (acc, from_left, from_right),
            (ext_shape,) + ((2, BLOCKS, size, WIDTH),) * 2 + ((RIM, WIDTH),),
        )
        up = shift(to_down, 1, 0)
        down = shift(to_up, -1, 0)
        total = four(total, tuple(zip(y_steps, x_steps))) + token
        total = four(total, tuple(zip(z_steps, y_steps)))
        ext, token = local_call(
            finish_kernel if last else update_kernel, "finish" if last else "update", (where,),
            (probe, ext, acc, up, down), (obj.shape if last else ext_shape, (RIM, WIDTH)),
        )
        here = total + swap(total, z_far, z_far) + token
        there = swap(total, *twin) + swap(total, z_twin, z_twin) + token
        halves = tuple(
            half - sums[:2] / (sums[2] + 1e-06) for half, sums in ((held, here), (spare, there))
        )
    held, other = halves
    probe = jnp.where(
        col % 2 == 0, jnp.concatenate([held, other], 1), jnp.concatenate([other, held], 1)
    )
    return ext, probe


def solution(mesh):
    in_specs = (
        P(None, "row", "col"),
        P(),
        P("row", "col", None, None, None),
        P(None, "row", "col", None),
        P(None, "row", "col", None),
    )
    out_specs = (P(None, "row", "col"), P())
    body = functools.partial(on_device, mesh.shape["row"], mesh.shape["col"])
    return jax.shard_map(
        body, mesh=mesh, in_specs=in_specs, out_specs=out_specs, check_vma=False
    )
```
